768 devices in a mesh: group: 64 (over y, x, core), member: 12 (over z).
Axes of the slice: x: 4, y: 8, z: 12, core: 2. Of those that a mesh axis runs over, the one named last changes fastest.
Arguments:
- state: bfloat16 [64, 12, 128, 9, 256], P('group', 'member'), may hold values from -6 to 6
- coef: bfloat16 [64, 12, 128, 256], P('group', 'member'), may hold values from 0.5 to 2
- new_group: int32 [64, 12, 128], P('group', 'member'), may hold values from -1 to 63, as said below
- face_lists: int32 [64, 12, 6, 128], P('group', 'member'), may hold values from -1 to 127
- lewis: float32 [9], replicated, may hold values from 0.3 to 3
Outputs:
- smoothed: float32 [64, 12, 128, 9, 256], P('group', 'member')
The draws below stay inside these ranges and needn't reach their ends.
Inputs may be any that keep to these rules, and one draw needn't show every extreme that they name: -1 marks an old slot that holds no patch. A patch keeps its member index. At most 2 patches go from one device to one device, and at most 128 arrive at one device. Counts, offsets and slot numbers derived from new_group may cross devices in any integer encoding.
All inputs are finite; a program needn't handle non-finite values.
Results may differ from the reference program's by a relative error of at most 0.0003.
Values may be sent and summed in bfloat16 or wider, within the bound.
A program may use at most 128 MiB of HBM per device.

```python
import math
import jax
import jax.numpy as jnp
from jax import lax

SPECIES = 9
PX = 16
PY = 16
SLOTS = 128
SWEEPS = 2
CELLS = 256
GROUPS = 64
MEMBERS = 12


def draw_new_group(key, part):
    key = jax.random.fold_in(key, 11)
    first, second, third, fourth = jax.random.split(key, 4)
    lane_shift = jax.random.randint(first, (MEMBERS,), 0, GROUPS)
    group_index = jnp.arange(GROUPS, dtype=jnp.int32)[:, None, None]
    slot_index = jnp.arange(SLOTS, dtype=jnp.int32)[None, None, :]
    dest = (group_index + slot_index + lane_shift[None, :, None]) % GROUPS
    busy = jax.random.randint(second, (MEMBERS, GROUPS), 0, 8) == 0
    forced = jax.random.randint(third, (MEMBERS,), 0, GROUPS)
    busy = busy | (jnp.arange(GROUPS, dtype=jnp.int32)[None, :] == forced[:, None])
    member_index = jnp.broadcast_to(jnp.arange(MEMBERS, dtype=jnp.int32)[None, :, None], dest.shape)
    hot = busy[member_index, dest]
    coin = jax.random.randint(fourth, dest.shape, 0, 2) == 0
    return jnp.where(hot | coin, dest, -1).astype(jnp.int32)


def touch_ends(array, key, least, top_value):
    longest = array.shape.index(max(array.shape))
    spots = []
    for shift in (0, 1):
        where = [jax.random.randint(jax.random.fold_in(key, axis), (), 0, length) for axis, length in enumerate(array.shape)]
        where[longest] = (where[longest] + shift) % array.shape[longest]
        spots.append(tuple(where))
    return array.at[spots[0]].set(least).at[spots[1]].set(top_value)


def block_scale(own_key, shape, shards, low, largest):
    def one(dim, blocks):
        steps = jax.random.uniform(jax.random.fold_in(jax.random.fold_in(own_key, 6), dim), (blocks,), jnp.float32, low / len(shards), largest / len(shards))
        return jnp.repeat(jnp.exp(steps), shape[dim] // blocks).reshape((-1,) + (1,) * (len(shape) - dim - 1))

    level = one(*shards[0])
    for cut in shards[1:]:
        level = level * one(*cut)
    return level


def normal_values(key, extent, width, limit, cuts=(), kind=jnp.bfloat16):
    drawn = width * jax.random.normal(key, extent, jnp.float32)
    if cuts:
        drawn = drawn * block_scale(key, extent, cuts, -0.22, 0.18)
    return jnp.clip(drawn, -limit, limit).astype(kind)


def setup_inputs(seed: int = 0) -> dict:
    key_list = jax.random.split(jax.random.key(seed), 6)
    state = normal_values(key_list[0], (GROUPS, MEMBERS, SLOTS, SPECIES, CELLS), 1.0, 6.0, ((0, 64), (1, 12)))
    coef = jnp.clip(jnp.exp(math.log(2.0) - 1.3862944 * jax.random.uniform(key_list[1], (GROUPS, MEMBERS, SLOTS, CELLS), jnp.float32) ** block_scale(key_list[1], (GROUPS, MEMBERS, SLOTS, CELLS), ((0, 64), (1, 12)), -0.2, 0.2)), 0.5, 2.0).astype(jnp.bfloat16)
    new_group = draw_new_group(jax.random.fold_in(key_list[5], 71), 0)
    face_lists = touch_ends(jax.random.randint(key_list[3], (GROUPS, MEMBERS, 6, SLOTS), -1, SLOTS), jax.random.fold_in(key_list[3], 1), -1, SLOTS - 1).astype(jnp.int32)
    lewis = jnp.clip(jnp.exp(jax.random.uniform(key_list[4], (SPECIES,), jnp.float32, math.log(0.3), math.log(3.0))), 0.3, 3.0)
    return dict(state=state, coef=coef, new_group=new_group, face_lists=face_lists, lewis=lewis)


def pick_rows(field, index):
    taken = jnp.take(field, jnp.clip(index, 0, field.shape[0] - 1), axis=0)
    return jnp.where((index >= 0)[:, None, None], taken, 0.0)


def beside_all(field, lists, lower, upper):
    count = field.shape[-1]
    span = lower.shape[-1]
    cell = jnp.arange(count, dtype=jnp.int32)
    xpos = cell % PX
    ypos = (cell // PX) % PY
    zpos = cell // span
    x_low = jnp.where(xpos == 0, jnp.roll(pick_rows(field, lists[0]), -(PX - 1), -1), jnp.roll(field, 1, -1))
    x_high = jnp.where(xpos == PX - 1, jnp.roll(pick_rows(field, lists[1]), PX - 1, -1), jnp.roll(field, -1, -1))
    y_low = jnp.where(ypos == 0, jnp.roll(pick_rows(field, lists[2]), -(PY - 1) * PX, -1), jnp.roll(field, PX, -1))
    y_high = jnp.where(ypos == PY - 1, jnp.roll(pick_rows(field, lists[3]), (PY - 1) * PX, -1), jnp.roll(field, -PX, -1))
    filler = jnp.zeros(field.shape[:-1] + (count - span,), jnp.float32)
    below = jnp.concatenate([pick_rows(lower, lists[4]), filler], -1)
    above = jnp.concatenate([filler, pick_rows(upper, lists[5])], -1)
    z_low = jnp.where(zpos == 0, below, jnp.roll(field, span, -1))
    z_high = jnp.where(zpos == count // span - 1, above, jnp.roll(field, -span, -1))
    return (x_low, x_high, y_low, y_high, z_low, z_high)


def sweep(phi, rhs, weights, lists, lower, upper, lewis):
    near = beside_all(phi, lists, lower, upper)
    flow = weights[0] * near[0]
    total = weights[0]
    for face in range(1, 6):
        flow = flow + weights[face] * near[face]
        total = total + weights[face]
    factor = lewis[:, None]
    return (rhs + factor * flow) / (1.0 + factor * total)


def stacked_faces(field):
    span = PX * PY
    tops = field[..., -span:]
    bottoms = field[..., :span]
    empty = jnp.zeros_like(tops[:1])
    return jnp.concatenate([empty, tops[:-1]], 0), jnp.concatenate([bottoms[1:], empty], 0)


def reference(state, coef, new_group, face_lists, lewis):
    groups, members, slots = new_group.shape
    valid = new_group >= 0
    onehot = (new_group[..., None] == jnp.arange(groups, dtype=jnp.int32)).astype(jnp.int32)
    lane = jnp.transpose(onehot, (1, 0, 2, 3)).reshape(members, groups * slots, groups)
    running = jnp.sum(jnp.cumsum(lane, 1) * lane, -1) - 1
    running = jnp.transpose(running.reshape(members, groups, slots), (1, 0, 2)).astype(jnp.int32)
    running = jnp.where(valid, running, slots).astype(jnp.int32)
    target = jnp.where(valid, new_group, groups).astype(jnp.int32)
    member_index = jnp.broadcast_to(jnp.arange(members, dtype=jnp.int32)[None, :, None], new_group.shape)
    rhs = jnp.zeros(state.shape, jnp.float32).at[target, member_index, running].set(state.astype(jnp.float32), mode="drop")
    new_coef = jnp.zeros(coef.shape, jnp.float32).at[target, member_index, running].set(coef.astype(jnp.float32), mode="drop")

    def one_group(items):
        rhs_g, coef_g, lists_g = items
        cell_coef = coef_g[:, :, None, :]
        coef_low, coef_high = stacked_faces(cell_coef)
        near = jax.vmap(beside_all)(cell_coef, lists_g, coef_low, coef_high)
        weights = tuple(0.5 * (cell_coef + item) for item in near)
        phi = rhs_g
        for step in range(SWEEPS):
            lower, upper = stacked_faces(phi)
            phi = jax.vmap(sweep, in_axes=(0, 0, 0, 0, 0, 0, None))(phi, rhs_g, weights, lists_g, lower, upper, lewis)
        return phi

    return lax.map(one_group, (rhs, new_coef, face_lists))
```

```python
import functools
import math

import jax
import jax.numpy as jnp
from jax import lax
from jax.experimental import pallas as pl
from jax.experimental.pallas import tpu as pltpu
from jax.sharding import PartitionSpec as P

LANES = 128
EDGE = 16
MESH = pl.DeviceIdType.MESH
F32 = jnp.float32
BF16 = jnp.bfloat16


def dot(left, right):
    return jnp.dot(left, right, preferred_element_type=F32)


def iota(shape, dim):
    return lax.broadcasted_iota(jnp.int32, shape, dim)


def ones_where(mask):
    return jnp.where(mask, 1.0, 0.0).astype(BF16)


def beside(field, picked):
    rows = field.shape[0]
    low, high = field[:, :LANES], field[:, LANES:]
    lane = iota((rows, LANES), 1)
    xpos = lane % EDGE

    def turn(part, by):
        return pltpu.roll(part, by % LANES, 1)

    def halves(part):
        return part[:, :LANES], part[:, LANES:]

    def both(one, two):
        return jnp.concatenate([one, two], axis=1)

    a, b = halves(picked[0])
    x_low = both(
        jnp.where(xpos == 0, turn(a, 1 - EDGE), turn(low, 1)),
        jnp.where(xpos == 0, turn(b, 1 - EDGE), turn(high, 1)),
    )
    a, b = halves(picked[1])
    x_high = both(
        jnp.where(xpos == EDGE - 1, turn(a, EDGE - 1), turn(low, -1)),
        jnp.where(xpos == EDGE - 1, turn(b, EDGE - 1), turn(high, -1)),
    )
    first = lane < EDGE
    low_up, high_up = turn(low, EDGE), turn(high, EDGE)
    y_low = both(
        jnp.where(first, turn(picked[2][:, LANES:], EDGE), low_up),
        jnp.where(first, low_up, high_up),
    )
    last = lane >= LANES - EDGE
    low_down, high_down = turn(low, -EDGE), turn(high, -EDGE)
    y_high = both(
        jnp.where(last, high_down, low_down),
        jnp.where(last, turn(picked[3][:, :LANES], -EDGE), high_down),
    )
    return x_low, x_high, y_low, y_high


def split(value):
    head = value.astype(BF16)
    return head, (value - head.astype(F32)).astype(BF16)


def kernel(
    across, along, members, per,
    dest_ref, lists_ref, lewis_ref, coef_ref, state_ref, out_ref,
    send1, recv1, send2, arrived, below, above, kept, weight, total, pick1, pick2, ghost, ghost_low, ghost_high,
    s1, r1, s2, r2, sz, rz, sp, rp,
):
    species, slots, cells = state_ref.shape
    chunks = (species + 1) // per
    group, member = lax.axis_index("group"), lax.axis_index("member")
    yme, xme = group // across, group % across
    upper, lower = lax.rem(member + 1, members), lax.rem(member + members - 1, members)
    xrows, yrows = 2 * along, 2 * across

    def xpeer(step):
        return lax.rem(xme + step, across)

    def ypeer(step):
        return lax.rem(yme + step, along)

    barrier = pltpu.get_barrier_semaphore()
    for step in range(1, across):
        pl.semaphore_signal(barrier, inc=1, device_id=(yme * across + xpeer(step), member), device_id_type=MESH)
    for step in range(1, along):
        pl.semaphore_signal(barrier, inc=1, device_id=(ypeer(step) * across + xme, member), device_id_type=MESH)
    pl.semaphore_signal(barrier, inc=1, device_id=(group, upper), device_id_type=MESH)
    pl.semaphore_signal(barrier, inc=1, device_id=(group, lower), device_id_type=MESH)

    row = iota((slots, slots), 0)
    col = iota((slots, slots), 1)
    earlier = ones_where(row < col)

    target = (row % xrows) // 2 * across + row // xrows
    match = ones_where(dest_ref[...] == target)
    rank = dot(match, earlier).astype(jnp.int32)
    chosen = ones_where((match > 0) & (rank == row % 2))
    source = (row % yrows) // 2 * xrows + row // yrows * 2 + row % 2
    swap = ones_where(source == col)

    pl.semaphore_wait(barrier, across + along)

    def xcopy(chunk, step):
        rows = pl.ds(pl.multiple_of(xpeer(step) * xrows, xrows), xrows)
        mine = pl.ds(pl.multiple_of(xme * xrows, xrows), xrows)
        part = pl.ds(chunk * per, per)
        return pltpu.make_async_remote_copy(
            src_ref=send1.at[part, rows], dst_ref=recv1.at[part, mine],
            send_sem=s1.at[chunk, step], recv_sem=r1.at[chunk, step],
            device_id=(yme * across + xpeer(step), member), device_id_type=MESH,
        )

    def ycopy(chunk, step):
        rows = pl.ds(pl.multiple_of(ypeer(step) * yrows, yrows), yrows)
        mine = pl.ds(pl.multiple_of(yme * yrows, yrows), yrows)
        part = pl.ds(chunk * per, per)
        return pltpu.make_async_remote_copy(
            src_ref=send2.at[part, rows], dst_ref=arrived.at[part, mine],
            send_sem=s2.at[chunk, step], recv_sem=r2.at[chunk, step],
            device_id=(ypeer(step) * across + xme, member), device_id_type=MESH,
        )

    def zcopies(chunk):
        part = pl.ds(chunk * per, per)
        return [
            pltpu.make_async_remote_copy(
                src_ref=arrived.at[part], dst_ref=place.at[part],
                send_sem=sz.at[chunk, way], recv_sem=rz.at[chunk, way],
                device_id=(group, to), device_id_type=MESH,
            )
            for way, (place, to) in enumerate(((below, upper), (above, lower)))
        ]

    def gcopies(kind):
        return [
            pltpu.make_async_remote_copy(
                src_ref=ghost.at[kind], dst_ref=place.at[kind],
                send_sem=sp.at[kind, way], recv_sem=rp.at[kind, way],
                device_id=(group, to), device_id_type=MESH,
            )
            for way, (place, to) in enumerate(((ghost_low, upper), (ghost_high, lower)))
        ]

    def pack(chunk, first):
        for j in range(per):
            plane = chunk * per + j
            block = coef_ref[...] if first and j == 0 else state_ref[plane - 1]
            send1[plane] = dot(chosen, block).astype(BF16)
        part = pl.ds(chunk * per, per)
        mine = pl.ds(pl.multiple_of(xme * xrows, xrows), xrows)
        recv1[part, mine, :] = send1[part, mine, :]
        for step in range(1, across):
            xcopy(chunk, step).start()

    def turn(chunk):
        for step in range(1, across):
            xcopy(chunk, step).wait_recv()
        for j in range(per):
            plane = chunk * per + j
            send2[plane] = dot(swap, recv1[plane]).astype(BF16)
        part = pl.ds(chunk * per, per)
        mine = pl.ds(pl.multiple_of(yme * yrows, yrows), yrows)
        arrived[part, mine, :] = send2[part, mine, :]
        for step in range(1, along):
            ycopy(chunk, step).start()

    def forward(chunk):
        for step in range(1, along):
            ycopy(chunk, step).wait_recv()
        for copy in zcopies(chunk):
            copy.start()

    pack(0, True)
    pl.loop(1, chunks)(lambda chunk: pack(chunk, False))
    turn(0)

    @pl.loop(1, chunks)
    def _(chunk):
        turn(chunk)
        forward(chunk - 1)

    forward(chunks - 1)

    lists = lists_ref[...]
    for face in range(6):
        entry = lists[face : face + 1]
        if face == 4:
            entry = jnp.where(member == 0, -1, entry)
        if face == 5:
            entry = jnp.where(member == members - 1, -1, entry)
        hot = jnp.where(entry == row, 1.0, 0.0).T.astype(BF16)
        pick2[face] = hot

    def placing(field):
        lead = ones_where(iota((8, cells), 1) == 0)
        value = lax.dot_general(lead, field, (((1,), (1,)), ((), ())), preferred_element_type=F32)
        there = ones_where(value > 0.25)
        place = dot(there, earlier)[0:1].astype(jnp.int32)
        return ones_where((place == row) & (there[0:1] > 0))

    for copy in zcopies(0):
        copy.wait_recv()
    order = placing(arrived[0])
    pick1[0] = order
    for face in range(4):
        pick1[face + 1] = dot(pick2[face], order).astype(BF16)
    pick1[5] = dot(pick2[4], placing(below[0])).astype(BF16)
    pick1[6] = dot(pick2[5], placing(above[0])).astype(BF16)

    def first_near(plane):
        block = arrived[plane]
        field = dot(pick1[0], block)
        near = beside(field, [dot(pick1[face + 1], block) for face in range(4)])
        return field, near + (dot(pick1[5], below[plane]), dot(pick1[6], above[plane]))

    field, near = first_near(0)
    summed = None
    for face in range(6):
        part = 0.5 * (field + near[face])
        weight[face] = part
        summed = part if summed is None else summed + part
    total[...] = summed

    def relax(kind, rhs, near):
        flow = weight[0] * near[0]
        for face in range(1, 6):
            flow = flow + weight[face] * near[face]
        factor = lewis_ref[kind]
        return (rhs + factor * flow) / (1.0 + factor * total[...])

    @pl.loop(0, species)
    def _(kind):
        plane = kind + 1

        @pl.when(plane % per == 0)
        def _():
            for copy in zcopies(plane // per):
                copy.wait_recv()

        rhs, near = first_near(plane)
        kept[kind] = rhs.astype(BF16)
        phi = relax(kind, rhs, near)
        out_ref[kind] = phi
        head, tail = split(phi)
        ghost[kind, :slots, :] = head
        ghost[kind, slots:, :] = tail
        for copy in gcopies(kind):
            copy.start()

    @pl.loop(0, species)
    def _(kind):
        phi = out_ref[kind]
        pair = ghost[kind]
        near = beside(
            phi, [dot(jnp.concatenate([pick2[face], pick2[face]], axis=1), pair) for face in range(4)]
        )
        for copy in gcopies(kind):
            copy.wait_recv()
        ends = tuple(
            dot(jnp.concatenate([pick2[face], pick2[face]], axis=1), place[kind])
            for face, place in ((4, ghost_low), (5, ghost_high))
        )
        out_ref[kind] = relax(kind, kept[kind].astype(F32), near + ends)

    @pl.loop(0, chunks)
    def _(chunk):
        for step in range(1, across):
            xcopy(chunk, step).wait_send()
        for step in range(1, along):
            ycopy(chunk, step).wait_send()
        for copy in zcopies(chunk):
            copy.wait_send()

    @pl.loop(0, species)
    def _(kind):
        for copy in gcopies(kind):
            copy.wait_send()


def per_device(across, along, members, state, coef, new_group, face_lists, lewis):
    _, _, slots, species, cells = state.shape
    per = 2
    chunks = (species + 1) // per
    whole = pl.BlockSpec(memory_space=pltpu.VMEM)
    dma = pltpu.SemaphoreType.DMA
    planes = (species + 1, slots, cells)
    out = pl.pallas_call(
        functools.partial(kernel, across, along, members, per),
        out_shape=jax.ShapeDtypeStruct((species, slots, cells), F32),
        in_specs=[whole, whole, pl.BlockSpec(memory_space=pltpu.SMEM), whole, whole],
        out_specs=whole,
        scratch_shapes=[
            pltpu.VMEM(planes, BF16),
            pltpu.VMEM(planes, BF16),
            pltpu.VMEM(planes, BF16),
            pltpu.VMEM(planes, BF16),
            pltpu.VMEM(planes, BF16),
            pltpu.VMEM(planes, BF16),
            pltpu.VMEM((species, slots, cells), BF16),
            pltpu.VMEM((6, slots, cells), F32),
            pltpu.VMEM((slots, cells), F32),
            pltpu.VMEM((7, slots, slots), BF16),
            pltpu.VMEM((6, slots, slots), BF16),
            pltpu.VMEM((species, 2 * slots, cells), BF16),
            pltpu.VMEM((species, 2 * slots, cells), BF16),
            pltpu.VMEM((species, 2 * slots, cells), BF16),
            dma((chunks, across)),
            dma((chunks, across)),
            dma((chunks, along)),
            dma((chunks, along)),
            dma((chunks, 2)),
            dma((chunks, 2)),
            dma((species, 2)),
            dma((species, 2)),
        ],
        compiler_params=pltpu.CompilerParams(
            collective_id=0, has_side_effects=True, vmem_limit_bytes=40 * 2**20
        ),
        name="regrid_and_sweep",
    )(
        new_group[0],
        face_lists[0, 0],
        lewis,
        coef[0, 0],
        jnp.transpose(state[0, 0], (1, 0, 2)),
    )
    return jnp.transpose(out, (1, 0, 2))[None, None]


def solution(mesh):
    groups, members = mesh.shape["group"], mesh.shape["member"]
    across = math.isqrt(groups)
    return jax.shard_map(
        functools.partial(per_device, across, groups // across, members),
        mesh=mesh,
        in_specs=(
            P("group", "member", None, None, None),
            P("group", "member", None, None),
            P("group", "member", None),
            P("group", "member", None, None),
            P(),
        ),
        out_specs=P("group", "member", None, None, None),
        check_vma=False,
    )
```

```python
import functools
import math

import jax
import jax.numpy as jnp
from jax import lax
from jax.experimental import pallas as pl
from jax.experimental.pallas import tpu as pltpu
from jax.sharding import PartitionSpec as P

LANES = 128
EDGE = 16
PER = 2
GROUP = 3
AHEAD = 3
BEHIND = 2
TOP = 32767.0
MESH = pl.DeviceIdType.MESH
F32 = jnp.float32
BF16 = jnp.bfloat16


def dot(left, right):
    return jnp.dot(left, right, preferred_element_type=F32)


def iota(shape, dim):
    return lax.broadcasted_iota(jnp.int32, shape, dim)


def ones_where(mask):
    return jnp.where(mask, 1.0, 0.0).astype(BF16)


def beside(field, picked):
    rows = field.shape[0]
    low, high = field[:, :LANES], field[:, LANES:]
    lane = iota((rows, LANES), 1)
    xpos = lane % EDGE

    def turn(part, by):
        return pltpu.roll(part, by % LANES, 1)

    def halves(part):
        return part[:, :LANES], part[:, LANES:]

    def both(one, two):
        return jnp.concatenate([one, two], axis=1)

    a, b = halves(picked[0])
    x_low = both(
        jnp.where(xpos == 0, turn(a, 1 - EDGE), turn(low, 1)),
        jnp.where(xpos == 0, turn(b, 1 - EDGE), turn(high, 1)),
    )
    a, b = halves(picked[1])
    x_high = both(
        jnp.where(xpos == EDGE - 1, turn(a, EDGE - 1), turn(low, -1)),
        jnp.where(xpos == EDGE - 1, turn(b, EDGE - 1), turn(high, -1)),
    )
    first = lane < EDGE
    low_up, high_up = turn(low, EDGE), turn(high, EDGE)
    y_low = both(
        jnp.where(first, turn(picked[2][:, LANES:], EDGE), low_up),
        jnp.where(first, low_up, high_up),
    )
    last = lane >= LANES - EDGE
    low_down, high_down = turn(low, -EDGE), turn(high, -EDGE)
    y_high = both(
        jnp.where(last, high_down, low_down),
        jnp.where(last, turn(picked[3][:, :LANES], -EDGE), high_down),
    )
    return x_low, x_high, y_low, y_high


def split(value):
    head = value.astype(BF16)
    return head, (value - head.astype(F32)).astype(BF16)


def kernel(
    across, along, members, per,
    dest_hbm, lists_hbm, lewis_hbm, coef_hbm, state_hbm, out_ref,
    dest_ref, lists_ref, lewis_ref, coef_ref, state_ref,
    send1, recv1, send2, arrived, below, above, kept, weight, total, pick1, pick2,
    code, code_low, code_high, scale, scale_low, scale_high,
    s0, s1, r1, s2, r2, sz, rz, sp, rp, sq, rq,
):
    species, slots, cells = state_ref.shape
    groups = species // GROUP
    chunks = (species + 1) // per
    group, member = lax.axis_index("group"), lax.axis_index("member")
    yme, xme = group // across, group % across
    has_upper, has_lower = member < members - 1, member > 0
    upper, lower = jnp.where(has_upper, member + 1, member - 1), jnp.where(has_lower, member - 1, member + 1)
    xrows, yrows = 2 * along, 2 * across

    xpeers = [lax.rem(xme + step, across) for step in range(1, across)]
    ypeers = [lax.rem(yme + step, along) for step in range(1, along)]
    xdevices = [yme * across + peer for peer in xpeers]
    ydevices = [peer * across + xme for peer in ypeers]

    barrier = pltpu.get_barrier_semaphore()
    for device in xdevices + ydevices:
        pl.semaphore_signal(barrier, inc=1, device_id=(device, member), device_id_type=MESH)

    @pl.when(has_upper)
    def _():
        pl.semaphore_signal(barrier, inc=1, device_id=(group, upper), device_id_type=MESH)

    @pl.when(has_lower)
    def _():
        pl.semaphore_signal(barrier, inc=1, device_id=(group, lower), device_id_type=MESH)

    loads = [
        pltpu.make_async_copy(here, there, s0.at[i])
        for i, (here, there) in enumerate((
            (dest_hbm, dest_ref), (coef_hbm, coef_ref), (state_hbm, state_ref),
            (lists_hbm, lists_ref), (lewis_hbm, lewis_ref),
        ))
    ]
    for load in loads:
        load.start()

    @pl.when(jnp.logical_not(has_lower))
    def _():
        below[...] = jnp.zeros_like(below)
        scale_low[...] = jnp.zeros_like(scale_low)
        code_low[...] = jnp.zeros_like(code_low)

    @pl.when(jnp.logical_not(has_upper))
    def _():
        above[...] = jnp.zeros_like(above)
        scale_high[...] = jnp.zeros_like(scale_high)
        code_high[...] = jnp.zeros_like(code_high)

    row = iota((slots, slots), 0)
    col = iota((slots, slots), 1)
    earlier = ones_where(row < col)

    target = (row % xrows) // 2 * across + row // xrows
    loads[0].wait()
    match = ones_where(dest_ref[...] == target)
    rank = dot(match, earlier).astype(jnp.int32)
    chosen = ones_where((match > 0) & (rank == row % 2))
    source = (row % yrows) // 2 * xrows + row // yrows * 2 + row % 2
    swap = ones_where(source == col)

    def blocks(peers, size):
        return [pl.ds(pl.multiple_of(peer * size, size), size) for peer in peers]

    xblocks, yblocks = blocks(xpeers, xrows), blocks(ypeers, yrows)
    (xmine,), (ymine,) = blocks([xme], xrows), blocks([yme], yrows)

    def send(chunk, here, there, mine, targets, sends, gets):
        part = pl.ds(chunk * per, per)
        for rows, device in targets:
            pltpu.make_async_remote_copy(
                src_ref=here.at[part, rows], dst_ref=there.at[part, mine],
                send_sem=sends.at[chunk], recv_sem=gets.at[chunk],
                device_id=(device, member), device_id_type=MESH,
            ).start()

    def wait(chunk, place, size, semaphores):
        others = place.at[pl.ds(chunk * per, per), pl.ds(0, slots - size)]
        pltpu.make_async_copy(others, others, semaphores.at[chunk]).wait()

    def zcopies(chunk):
        part = pl.ds(chunk * per, per)
        return [
            (arrived.at[part], place.at[part], sz.at[chunk, way], rz.at[chunk, way], way)
            for way, place in enumerate((below, above))
        ]

    def gcopies(part):
        return [
            (here.at[span], place.at[span], sends.at[part, way], gets.at[part, way], way)
            for here, places, sends, gets, span in (
                (code, (code_low, code_high), sp, rp, pl.ds(part * GROUP, GROUP)),
                (scale, (scale_low, scale_high), sq, rq, part),
            )
            for way, place in enumerate(places)
        ]

    def along_z(copies, act):
        for here, place, send, get, way in copies:
            copy = pltpu.make_async_remote_copy(
                src_ref=here, dst_ref=place, send_sem=send, recv_sem=get,
                device_id=(group, lower if way else upper), device_id_type=MESH,
            )
            there = has_lower if (act == "wait_recv") != (way == 1) else has_upper
            pl.when(there)(getattr(copy, act))

    def pack(chunk, first):
        for j in range(per):
            plane = chunk * per + j
            block = coef_ref[...] if first and j == 0 else state_ref[plane - 1]
            send1[plane] = dot(chosen, block).astype(BF16)
        part = pl.ds(chunk * per, per)
        recv1[part, xmine, :] = send1[part, xmine, :]

    def spread(chunk):
        send(chunk, send1, recv1, xmine, list(zip(xblocks, xdevices)), s1, r1)

    def turn(chunk):
        wait(chunk, recv1, xrows, r1)
        for j in range(per):
            plane = chunk * per + j
            send2[plane] = dot(swap, recv1[plane]).astype(BF16)
        send(chunk, send2, arrived, ymine, list(zip(yblocks, ydevices)), s2, r2)
        part = pl.ds(chunk * per, per)
        arrived[part, ymine, :] = send2[part, ymine, :]

    def forward(chunk):
        wait(chunk, arrived, yrows, r2)
        along_z(zcopies(chunk), "start")

    loads[1].wait()
    loads[2].wait()
    pack(0, True)
    loads[3].wait()
    loads[4].wait()
    for face in range(6):
        pick2[face] = jnp.where(lists_ref[face] == row, 1.0, 0.0).T.astype(BF16)
    pl.semaphore_wait(
        barrier, across + along - 2 + has_upper.astype(jnp.int32) + has_lower.astype(jnp.int32)
    )
    spread(0)

    def placing(field):
        lead = ones_where(iota((8, cells), 1) == 0)
        value = lax.dot_general(lead, field, (((1,), (1,)), ((), ())), preferred_element_type=F32)
        there = ones_where(value > 0.25)
        place = dot(there, earlier)[0:1].astype(jnp.int32)
        return ones_where((place == row) & (there[0:1] > 0))

    def first_near(plane):
        block = arrived[plane]
        field = dot(pick1[0], block)
        near = beside(field, [dot(pick1[face + 1], block) for face in range(4)])
        return field, near + (dot(pick1[5], below[plane]), dot(pick1[6], above[plane]))

    def setup():
        order = placing(arrived[0])
        pick1[0] = order
        for face in range(4):
            pick1[face + 1] = dot(pick2[face], order).astype(BF16)
        pick1[5] = dot(pick2[4], placing(below[0])).astype(BF16)
        pick1[6] = dot(pick2[5], placing(above[0])).astype(BF16)

        field, near = first_near(0)
        summed = None
        for face in range(6):
            part = 0.5 * (field + near[face])
            weight[face] = part
            summed = part if summed is None else summed + part
        total[...] = summed

    def relax(kind, rhs, near):
        flow = weight[0] * near[0]
        for face in range(1, 6):
            flow = flow + weight[face] * near[face]
        factor = lewis_ref[kind]
        return (rhs + factor * flow) / (1.0 + factor * total[...])

    def relax_first(plane):
        kind = plane - 1
        rhs, near = first_near(plane)
        kept[kind] = rhs.astype(BF16)
        phi = relax(kind, rhs, near)
        out_ref[kind] = phi
        largest = jnp.maximum(jnp.max(jnp.abs(phi), axis=1, keepdims=True), 1e-30)
        unit = (largest * (1.01 / TOP)).astype(BF16).astype(F32)
        code[kind] = jnp.round(phi * (1.0 / unit)).astype(jnp.int32).astype(jnp.int16)
        part = kind // GROUP
        across_lanes = dot(jnp.ones((16, slots), BF16), jnp.where(row == col, unit, 0.0).astype(BF16))
        scale[part, pl.ds(kind % GROUP, 1), :] = across_lanes[:1]

        @pl.when(kind % GROUP == GROUP - 1)
        def _():
            along_z(gcopies(part), "start")

    @pl.loop(1, chunks + AHEAD + 1 + BEHIND)
    def _(step):
        @pl.when(step < chunks)
        def _():
            pack(step, False)
            spread(step)

        @pl.when((step >= AHEAD) & (step < chunks + AHEAD))
        def _():
            turn(step - AHEAD)

        @pl.when((step >= AHEAD + 1) & (step < chunks + AHEAD + 1))
        def _():
            forward(step - AHEAD - 1)

        @pl.when(step >= AHEAD + 1 + BEHIND)
        def _():
            chunk = step - AHEAD - 1 - BEHIND
            along_z(zcopies(chunk), "wait_recv")
            pl.when(chunk == 0)(setup)
            pl.loop(jnp.where(chunk == 0, 1, chunk * per), chunk * per + per)(relax_first)

    @pl.loop(0, chunks)
    def _(chunk):
        wait(chunk, send1, xrows, s1)
        wait(chunk, send2, yrows, s2)
        along_z(zcopies(chunk), "wait_send")

    @pl.loop(0, species)
    def _(kind):
        phi = out_ref[kind]
        head, tail = split(phi)
        pair = jnp.concatenate([head, tail], axis=0)
        near = beside(
            phi, [dot(jnp.concatenate([pick2[face], pick2[face]], axis=1), pair) for face in range(4)]
        )
        part = kind // GROUP

        @pl.when(kind % GROUP == 0)
        def _():
            along_z(gcopies(part), "wait_recv")

        ends = ()
        for face, codes, scales in ((4, code_low, scale_low), (5, code_high, scale_high)):
            value = codes[kind].astype(jnp.int32).astype(F32)
            high = jnp.floor(value * (1.0 / 256.0) + 0.5)
            pair = jnp.concatenate([high.astype(BF16), (value - 256.0 * high).astype(BF16)], axis=0)
            hot = pick2[face].astype(F32) * scales[part, pl.ds(kind % GROUP, 1), :]
            ends += (dot(jnp.concatenate([(256.0 * hot).astype(BF16), hot.astype(BF16)], axis=1), pair),)
        out_ref[kind] = relax(kind, kept[kind].astype(F32), near + ends)

    @pl.loop(0, groups)
    def _(part):
        along_z(gcopies(part), "wait_send")


def per_device(across, along, members, state, coef, new_group, face_lists, lewis):
    _, _, slots, species, cells = state.shape
    per = PER
    chunks = (species + 1) // per
    whole = pl.BlockSpec(memory_space=pltpu.VMEM)
    far = pl.BlockSpec(memory_space=pltpu.HBM)
    groups = species // GROUP
    dma = pltpu.SemaphoreType.DMA
    planes = (species + 1, slots, cells)
    out = pl.pallas_call(
        functools.partial(kernel, across, along, members, per),
        out_shape=jax.ShapeDtypeStruct((species, slots, cells), F32),
        in_specs=[far] * 5,
        out_specs=whole,
        scratch_shapes=[
            pltpu.VMEM((1, slots), jnp.int32),
            pltpu.VMEM((6, 1, slots), jnp.int32),
            pltpu.SMEM((species,), F32),
            pltpu.VMEM((slots, cells), BF16),
            pltpu.VMEM((species, slots, cells), BF16),
            pltpu.VMEM(planes, BF16),
            pltpu.VMEM(planes, BF16),
            pltpu.VMEM(planes, BF16),
            pltpu.VMEM(planes, BF16),
            pltpu.VMEM(planes, BF16),
            pltpu.VMEM(planes, BF16),
            pltpu.VMEM((species, slots, cells), BF16),
            pltpu.VMEM((6, slots, cells), F32),
            pltpu.VMEM((slots, cells), F32),
            pltpu.VMEM((7, slots, slots), BF16),
            pltpu.VMEM((6, slots, slots), BF16),
            pltpu.VMEM((species, slots, cells), jnp.int16),
            pltpu.VMEM((species, slots, cells), jnp.int16),
            pltpu.VMEM((species, slots, cells), jnp.int16),
            pltpu.VMEM((groups, 8, slots), F32),
            pltpu.VMEM((groups, 8, slots), F32),
            pltpu.VMEM((groups, 8, slots), F32),
            dma((5,)),
            dma((chunks,)),
            dma((chunks,)),
            dma((chunks,)),
            dma((chunks,)),
            dma((chunks, 2)),
            dma((chunks, 2)),
            dma((groups, 2)),
            dma((groups, 2)),
            dma((groups, 2)),
            dma((groups, 2)),
        ],
        compiler_params=pltpu.CompilerParams(
            collective_id=0, has_side_effects=True, vmem_limit_bytes=60 * 2**20
        ),
        name="regrid_and_sweep",
    )(
        new_group[0],
        jnp.transpose(face_lists[0], (1, 0, 2)),
        lewis,
        coef[0, 0],
        jnp.transpose(state[0, 0], (1, 0, 2)),
    )
    return jnp.transpose(out, (1, 0, 2))[None, None]


def solution(mesh):
    groups, members = mesh.shape["group"], mesh.shape["member"]
    across = math.isqrt(groups)
    return jax.shard_map(
        functools.partial(per_device, across, groups // across, members),
        mesh=mesh,
        in_specs=(
            P("group", "member", None, None, None),
            P("group", "member", None, None),
            P("group", "member", None),
            P("group", "member", None, None),
            P(),
        ),
        out_specs=P("group", "member", None, None, None),
        check_vma=False,
    )
```

```python
import functools
import math

import jax
import jax.numpy as jnp
from jax import lax
from jax.experimental import pallas as pl
from jax.experimental.pallas import tpu as pltpu
from jax.sharding import PartitionSpec as P

LANES = 128
EDGE = 16
SIZES = (1, 2, 2, 2, 3)
GROUP = 3
AHEAD = 2
LAG = 1
BEHIND = 2
TOP = 32767.0
MESH = pl.DeviceIdType.MESH
F32 = jnp.float32
BF16 = jnp.bfloat16


def dot(left, right):
    return jnp.dot(left, right, preferred_element_type=F32)


def iota(shape, dim):
    return lax.broadcasted_iota(jnp.int32, shape, dim)


def ones_where(mask):
    return jnp.where(mask, 1.0, 0.0).astype(BF16)


def beside(field, picked):
    rows = field.shape[0]
    low, high = field[:, :LANES], field[:, LANES:]
    lane = iota((rows, LANES), 1)
    xpos = lane % EDGE

    def turn(part, by):
        return pltpu.roll(part, by % LANES, 1)

    def halves(part):
        return part[:, :LANES], part[:, LANES:]

    def both(one, two):
        return jnp.concatenate([one, two], axis=1)

    a, b = halves(picked[0])
    x_low = both(
        jnp.where(xpos == 0, turn(a, 1 - EDGE), turn(low, 1)),
        jnp.where(xpos == 0, turn(b, 1 - EDGE), turn(high, 1)),
    )
    a, b = halves(picked[1])
    x_high = both(
        jnp.where(xpos == EDGE - 1, turn(a, EDGE - 1), turn(low, -1)),
        jnp.where(xpos == EDGE - 1, turn(b, EDGE - 1), turn(high, -1)),
    )
    first = lane < EDGE
    low_up, high_up = turn(low, EDGE), turn(high, EDGE)
    y_low = both(
        jnp.where(first, turn(picked[2][:, LANES:], EDGE), low_up),
        jnp.where(first, low_up, high_up),
    )
    last = lane >= LANES - EDGE
    low_down, high_down = turn(low, -EDGE), turn(high, -EDGE)
    y_high = both(
        jnp.where(last, high_down, low_down),
        jnp.where(last, turn(picked[3][:, :LANES], -EDGE), high_down),
    )
    return x_low, x_high, y_low, y_high


def split(value):
    head = value.astype(BF16)
    return head, (value - head.astype(F32)).astype(BF16)


def kernel(
    across, along, members, sizes,
    dest_hbm, lists_hbm, lewis_hbm, coef_hbm, state_hbm, out_ref,
    dest_ref, lists_ref, lewis_ref, coef_ref, state_ref,
    send1, recv1, send2, arrived, below, above, kept, weight, total, pick1, pick2,
    code, code_low, code_high, scale, scale_low, scale_high,
    s0, s1, r1, s2, r2, sz, rz, sp, rp, sq, rq,
):
    species, slots, cells = state_ref.shape
    groups = species // GROUP
    chunks = len(sizes)
    parts = [pl.ds(sum(sizes[:chunk]), sizes[chunk]) for chunk in range(chunks)]
    group, member = lax.axis_index("group"), lax.axis_index("member")
    yme, xme = group // across, group % across
    has_upper, has_lower = member < members - 1, member > 0
    upper, lower = jnp.where(has_upper, member + 1, member - 1), jnp.where(has_lower, member - 1, member + 1)
    xrows, yrows = 2 * along, 2 * across

    xpeers = [lax.rem(xme + step, across) for step in range(1, across)]
    ypeers = [lax.rem(yme + step, along) for step in range(1, along)]
    xdevices = [yme * across + peer for peer in xpeers]
    ydevices = [peer * across + xme for peer in ypeers]

    loads = [
        pltpu.make_async_copy(here, there, s0.at[i])
        for i, (here, there) in enumerate((
            (dest_hbm, dest_ref), (coef_hbm, coef_ref), (state_hbm, state_ref),
            (lists_hbm, lists_ref), (lewis_hbm, lewis_ref),
        ))
    ]
    for load in loads:
        load.start()

    barrier = pltpu.get_barrier_semaphore()
    for device in xdevices + ydevices:
        pl.semaphore_signal(barrier, inc=1, device_id=(device, member), device_id_type=MESH)

    @pl.when(has_upper)
    def _():
        pl.semaphore_signal(barrier, inc=1, device_id=(group, upper), device_id_type=MESH)

    @pl.when(has_lower)
    def _():
        pl.semaphore_signal(barrier, inc=1, device_id=(group, lower), device_id_type=MESH)

    row = iota((slots, slots), 0)
    col = iota((slots, slots), 1)
    earlier = ones_where(row < col)

    target = (row % xrows) // 2 * across + row // xrows
    loads[0].wait()
    match = ones_where(dest_ref[...] == target)
    rank = dot(match, earlier).astype(jnp.int32)
    chosen = ones_where((match > 0) & (rank == row % 2))
    source = (row % yrows) // 2 * xrows + row // yrows * 2 + row % 2
    swap = ones_where(source == col)

    def blocks(peers, size):
        return [pl.ds(pl.multiple_of(peer * size, size), size) for peer in peers]

    xblocks, yblocks = blocks(xpeers, xrows), blocks(ypeers, yrows)
    (xmine,), (ymine,) = blocks([xme], xrows), blocks([yme], yrows)

    def send(chunk, here, there, mine, targets, sends, gets):
        part = parts[chunk]
        for rows, device in targets:
            pltpu.make_async_remote_copy(
                src_ref=here.at[part, rows], dst_ref=there.at[part, mine],
                send_sem=sends.at[chunk], recv_sem=gets.at[chunk],
                device_id=(device, member), device_id_type=MESH,
            ).start()

    def wait(chunk, place, size, semaphores):
        others = place.at[parts[chunk], pl.ds(0, slots - size)]
        pltpu.make_async_copy(others, others, semaphores.at[chunk]).wait()

    def zcopies(chunk):
        part = parts[chunk]
        return [
            (arrived.at[part], place.at[part], sz.at[chunk, way], rz.at[chunk, way], way)
            for way, place in enumerate((below, above))
        ]

    def gcopies(part):
        return [
            (here.at[span], place.at[span], sends.at[part, way], gets.at[part, way], way)
            for here, places, sends, gets, span in (
                (code, (code_low, code_high), sp, rp, pl.ds(part * GROUP, GROUP)),
                (scale, (scale_low, scale_high), sq, rq, part),
            )
            for way, place in enumerate(places)
        ]

    def along_z(copies, act):
        for here, place, send, get, way in copies:
            copy = pltpu.make_async_remote_copy(
                src_ref=here, dst_ref=place, send_sem=send, recv_sem=get,
                device_id=(group, lower if way else upper), device_id_type=MESH,
            )
            there = has_lower if (act == "wait_recv") != (way == 1) else has_upper
            pl.when(there)(getattr(copy, act))

    def pack(chunk):
        for plane in range(parts[chunk].start, parts[chunk].start + parts[chunk].size):
            block = state_ref[plane - 1] if plane else coef_ref[...]
            send1[plane] = dot(chosen, block).astype(BF16)
        part = parts[chunk]
        recv1[part, xmine, :] = send1[part, xmine, :]

    def spread(chunk):
        send(chunk, send1, recv1, xmine, list(zip(xblocks, xdevices)), s1, r1)

    def turn(chunk):
        wait(chunk, recv1, xrows, r1)
        for plane in range(parts[chunk].start, parts[chunk].start + parts[chunk].size):
            send2[plane] = dot(swap, recv1[plane]).astype(BF16)
        send(chunk, send2, arrived, ymine, list(zip(yblocks, ydevices)), s2, r2)
        part = parts[chunk]
        arrived[part, ymine, :] = send2[part, ymine, :]

    def forward(chunk):
        wait(chunk, arrived, yrows, r2)
        along_z(zcopies(chunk), "start")

    def start(chunk):
        pack(chunk)
        spread(chunk)

    loads[1].wait()
    pack(0)
    pl.semaphore_wait(
        barrier, across + along - 2 + has_upper.astype(jnp.int32) + has_lower.astype(jnp.int32)
    )
    spread(0)
    loads[2].wait()
    start(1)

    loads[3].wait()
    loads[4].wait()
    for face in range(6):
        pick2[face] = jnp.where(lists_ref[face] == row, 1.0, 0.0).T.astype(BF16)

    @pl.when(jnp.logical_not(has_lower))
    def _():
        below[...] = jnp.zeros_like(below)
        scale_low[...] = jnp.zeros_like(scale_low)
        code_low[...] = jnp.zeros_like(code_low)

    @pl.when(jnp.logical_not(has_upper))
    def _():
        above[...] = jnp.zeros_like(above)
        scale_high[...] = jnp.zeros_like(scale_high)
        code_high[...] = jnp.zeros_like(code_high)

    def placing(field):
        lead = ones_where(iota((8, cells), 1) == 0)
        value = lax.dot_general(lead, field, (((1,), (1,)), ((), ())), preferred_element_type=F32)
        there = ones_where(value > 0.25)
        place = dot(there, earlier)[0:1].astype(jnp.int32)
        return ones_where((place == row) & (there[0:1] > 0))

    def first_near(plane):
        block = arrived[plane]
        field = dot(pick1[0], block)
        near = beside(field, [dot(pick1[face + 1], block) for face in range(4)])
        return field, near + (dot(pick1[5], below[plane]), dot(pick1[6], above[plane]))

    def setup():
        order = placing(arrived[0])
        pick1[0] = order
        for face in range(4):
            pick1[face + 1] = dot(pick2[face], order).astype(BF16)
        pick1[5] = dot(pick2[4], placing(below[0])).astype(BF16)
        pick1[6] = dot(pick2[5], placing(above[0])).astype(BF16)

        field, near = first_near(0)
        summed = None
        for face in range(6):
            part = 0.5 * (field + near[face])
            weight[face] = part
            summed = part if summed is None else summed + part
        total[...] = summed

    def relax(kind, rhs, near, faces):
        flow = None
        for face, value in zip(faces, near):
            part = weight[face] * value
            flow = part if flow is None else flow + part
        factor = lewis_ref[kind]
        share = 1.0 / (1.0 + factor * total[...])
        return rhs * share + (factor * share) * flow if rhs is not None else (factor * share) * flow

    def relax_first(plane):
        kind = plane - 1
        rhs, near = first_near(plane)
        kept[kind] = rhs.astype(BF16)
        phi = relax(kind, rhs, near, range(6))
        out_ref[kind] = phi
        largest = jnp.maximum(jnp.max(jnp.abs(phi), axis=1, keepdims=True), 1e-30)
        unit = (largest * (1.01 / TOP)).astype(BF16).astype(F32)
        code[kind] = jnp.round(phi * (1.0 / unit)).astype(jnp.int32).astype(jnp.int16)
        part = kind // GROUP
        across_lanes = dot(jnp.ones((16, slots), BF16), jnp.where(row == col, unit, 0.0).astype(BF16))
        scale[part, pl.ds(kind % GROUP, 1), :] = across_lanes[:1]

        @pl.when(kind % GROUP == GROUP - 1)
        def _():
            along_z(gcopies(part), "start")

    def sweep(chunk):
        along_z(zcopies(chunk), "wait_recv")
        if chunk == 0:
            setup()
        first = parts[chunk].start
        pl.loop(max(first, 1), first + parts[chunk].size)(relax_first)

    for step in range(2, chunks + AHEAD + LAG + BEHIND):
        if step < chunks:
            start(step)
        if 0 <= step - AHEAD < chunks:
            turn(step - AHEAD)
        if 0 <= step - AHEAD - LAG < chunks:
            forward(step - AHEAD - LAG)
        chunk = step - AHEAD - LAG - BEHIND
        if 0 <= chunk < chunks:
            sweep(chunk)

    for chunk in range(chunks):
        wait(chunk, send1, xrows, s1)
        wait(chunk, send2, yrows, s2)
        along_z(zcopies(chunk), "wait_send")

    @pl.loop(0, species)
    def _(kind):
        phi = out_ref[kind]
        head, tail = split(phi)
        pair = jnp.concatenate([head, tail], axis=0)
        near = beside(
            phi, [dot(jnp.concatenate([pick2[face], pick2[face]], axis=1), pair) for face in range(4)]
        )
        out_ref[kind] = relax(kind, kept[kind].astype(F32), near, range(4))

    @pl.loop(0, species)
    def _(kind):
        part = kind // GROUP

        @pl.when(kind % GROUP == 0)
        def _():
            along_z(gcopies(part), "wait_recv")

        ends = ()
        for face, codes, scales in ((4, code_low, scale_low), (5, code_high, scale_high)):
            value = codes[kind].astype(jnp.int32).astype(F32)
            high = jnp.floor(value * (1.0 / 256.0) + 0.5)
            pair = jnp.concatenate([high.astype(BF16), (value - 256.0 * high).astype(BF16)], axis=0)
            hot = pick2[face].astype(F32) * scales[part, pl.ds(kind % GROUP, 1), :]
            ends += (dot(jnp.concatenate([(256.0 * hot).astype(BF16), hot.astype(BF16)], axis=1), pair),)
        out_ref[kind] = out_ref[kind] + relax(kind, None, ends, (4, 5))

    @pl.loop(0, groups)
    def _(part):
        along_z(gcopies(part), "wait_send")


def per_device(across, along, members, state, coef, new_group, face_lists, lewis):
    _, _, slots, species, cells = state.shape
    chunks = len(SIZES)
    whole = pl.BlockSpec(memory_space=pltpu.VMEM)
    far = pl.BlockSpec(memory_space=pltpu.HBM)
    groups = species // GROUP
    dma = pltpu.SemaphoreType.DMA
    planes = (species + 1, slots, cells)
    out = pl.pallas_call(
        functools.partial(kernel, across, along, members, SIZES),
        out_shape=pltpu.VMEM((species, slots, cells), F32),
        in_specs=[far] * 5,
        out_specs=whole,
        scratch_shapes=[
            pltpu.VMEM((1, slots), jnp.int32),
            pltpu.VMEM((6, 1, slots), jnp.int32),
            pltpu.SMEM((species,), F32),
            pltpu.VMEM((slots, cells), BF16),
            pltpu.VMEM((species, slots, cells), BF16),
            pltpu.VMEM(planes, BF16),
            pltpu.VMEM(planes, BF16),
            pltpu.VMEM(planes, BF16),
            pltpu.VMEM(planes, BF16),
            pltpu.VMEM(planes, BF16),
            pltpu.VMEM(planes, BF16),
            pltpu.VMEM((species, slots, cells), BF16),
            pltpu.VMEM((6, slots, cells), F32),
            pltpu.VMEM((slots, cells), F32),
            pltpu.VMEM((7, slots, slots), BF16),
            pltpu.VMEM((6, slots, slots), BF16),
            pltpu.VMEM((species, slots, cells), jnp.int16),
            pltpu.VMEM((species, slots, cells), jnp.int16),
            pltpu.VMEM((species, slots, cells), jnp.int16),
            pltpu.VMEM((groups, 8, slots), F32),
            pltpu.VMEM((groups, 8, slots), F32),
            pltpu.VMEM((groups, 8, slots), F32),
            dma((5,)),
            dma((chunks,)),
            dma((chunks,)),
            dma((chunks,)),
            dma((chunks,)),
            dma((chunks, 2)),
            dma((chunks, 2)),
            dma((groups, 2)),
            dma((groups, 2)),
            dma((groups, 2)),
            dma((groups, 2)),
        ],
        compiler_params=pltpu.CompilerParams(
            collective_id=0, has_side_effects=True, vmem_limit_bytes=60 * 2**20
        ),
        name="regrid_and_sweep",
    )(
        new_group[0],
        jnp.transpose(face_lists[0], (1, 0, 2)),
        lewis,
        coef[0, 0],
        jnp.transpose(state[0, 0], (1, 0, 2)),
    )
    return jnp.transpose(out, (1, 0, 2))[None, None]


def solution(mesh):
    groups, members = mesh.shape["group"], mesh.shape["member"]
    across = math.isqrt(groups)
    return jax.shard_map(
        functools.partial(per_device, across, groups // across, members),
        mesh=mesh,
        in_specs=(
            P("group", "member", None, None, None),
            P("group", "member", None, None),
            P("group", "member", None),
            P("group", "member", None, None),
            P(),
        ),
        out_specs=P("group", "member", None, None, None),
        check_vma=False,
    )
```

```python
import functools
import math

import jax
import jax.numpy as jnp
from jax import lax
from jax.experimental import pallas as pl
from jax.experimental.pallas import tpu as pltpu
from jax.sharding import PartitionSpec as P

LANES = 128
EDGE = 16
SIZES = (1, 2, 2, 2, 3)
EARLY = 4
BEHIND = 2
TOP = 32767.0
MESH = pl.DeviceIdType.MESH
F32 = jnp.float32
BF16 = jnp.bfloat16


def dot(left, right):
    return jnp.dot(left, right, preferred_element_type=F32)


def iota(shape, dim):
    return lax.broadcasted_iota(jnp.int32, shape, dim)


def ones_where(mask):
    return jnp.where(mask, 1.0, 0.0).astype(BF16)


def beside(field, picked):
    rows = field.shape[0]
    low, high = field[:, :LANES], field[:, LANES:]
    lane = iota((rows, LANES), 1)
    xpos = lane % EDGE

    def turn(part, by):
        return pltpu.roll(part, by % LANES, 1)

    def halves(part):
        return part[:, :LANES], part[:, LANES:]

    def both(one, two):
        return jnp.concatenate([one, two], axis=1)

    a, b = halves(picked[0])
    x_low = both(
        jnp.where(xpos == 0, turn(a, 1 - EDGE), turn(low, 1)),
        jnp.where(xpos == 0, turn(b, 1 - EDGE), turn(high, 1)),
    )
    a, b = halves(picked[1])
    x_high = both(
        jnp.where(xpos == EDGE - 1, turn(a, EDGE - 1), turn(low, -1)),
        jnp.where(xpos == EDGE - 1, turn(b, EDGE - 1), turn(high, -1)),
    )
    first = lane < EDGE
    low_up, high_up = turn(low, EDGE), turn(high, EDGE)
    y_low = both(
        jnp.where(first, turn(picked[2][:, LANES:], EDGE), low_up),
        jnp.where(first, low_up, high_up),
    )
    last = lane >= LANES - EDGE
    low_down, high_down = turn(low, -EDGE), turn(high, -EDGE)
    y_high = both(
        jnp.where(last, high_down, low_down),
        jnp.where(last, turn(picked[3][:, :LANES], -EDGE), high_down),
    )
    return x_low, x_high, y_low, y_high


def split(value):
    head = value.astype(BF16)
    return head, (value - head.astype(F32)).astype(BF16)


def kernel(
    across, along, members, sizes,
    dest_hbm, lists_hbm, lewis_hbm, coef_hbm, state_hbm, out_ref,
    dest_ref, lists_ref, lewis_ref, coef_ref, state_ref,
    send1, recv1, send2, arrived, below, above, kept, weight, total, pick1, pick2,
    code, code_low, code_high, scale, scale_low, scale_high,
    s0, s1, r1, s2, r2, sz, rz, sp, rp, sq, rq,
):
    species, slots, cells = state_ref.shape
    chunks = len(sizes)
    parts = [pl.ds(sum(sizes[:chunk]), sizes[chunk]) for chunk in range(chunks)]
    group, member = lax.axis_index("group"), lax.axis_index("member")
    yme, xme = group // across, group % across
    has_upper, has_lower = member < members - 1, member > 0
    upper, lower = jnp.where(has_upper, member + 1, member - 1), jnp.where(has_lower, member - 1, member + 1)
    xrows, yrows = 2 * along, 2 * across

    xpeers = [lax.rem(xme + step, across) for step in range(1, across)]
    ypeers = [lax.rem(yme + step, along) for step in range(1, along)]
    xdevices = [yme * across + peer for peer in xpeers]
    ydevices = [peer * across + xme for peer in ypeers]

    loads = [
        pltpu.make_async_copy(here, there, s0.at[i])
        for i, (here, there) in enumerate((
            (dest_hbm, dest_ref), (coef_hbm, coef_ref), (state_hbm, state_ref),
            (lists_hbm, lists_ref), (lewis_hbm, lewis_ref),
        ))
    ]
    for load in loads:
        load.start()

    barrier = pltpu.get_barrier_semaphore()
    for device in xdevices + ydevices:
        pl.semaphore_signal(barrier, inc=1, device_id=(device, member), device_id_type=MESH)

    @pl.when(has_upper)
    def _():
        pl.semaphore_signal(barrier, inc=1, device_id=(group, upper), device_id_type=MESH)

    @pl.when(has_lower)
    def _():
        pl.semaphore_signal(barrier, inc=1, device_id=(group, lower), device_id_type=MESH)

    row = iota((slots, slots), 0)
    col = iota((slots, slots), 1)
    earlier = ones_where(row < col)

    target = (row % xrows) // 2 * across + row // xrows
    loads[0].wait()
    match = ones_where(dest_ref[...] == target)
    rank = dot(match, earlier).astype(jnp.int32)
    chosen = ones_where((match > 0) & (rank == row % 2))
    source = (row % yrows) // 2 * xrows + row // yrows * 2 + row % 2
    swap = ones_where(source == col)

    def blocks(peers, size):
        return [pl.ds(pl.multiple_of(peer * size, size), size) for peer in peers]

    xblocks, yblocks = blocks(xpeers, xrows), blocks(ypeers, yrows)
    (xmine,), (ymine,) = blocks([xme], xrows), blocks([yme], yrows)

    def send(chunk, here, there, mine, targets, sends, gets):
        part = parts[chunk]
        for rows, device in targets:
            pltpu.make_async_remote_copy(
                src_ref=here.at[part, rows], dst_ref=there.at[part, mine],
                send_sem=sends.at[chunk], recv_sem=gets.at[chunk],
                device_id=(device, member), device_id_type=MESH,
            ).start()

    def wait(chunk, place, size, semaphores):
        others = place.at[parts[chunk], pl.ds(0, slots - size)]
        pltpu.make_async_copy(others, others, semaphores.at[chunk]).wait()

    def kinds(chunk):
        first = max(parts[chunk].start, 1)
        return pl.ds(first - 1, parts[chunk].start + parts[chunk].size - first)

    def zcopies(chunk):
        part = parts[chunk]
        return [
            (arrived.at[part], place.at[part], sz.at[chunk, way], rz.at[chunk, way], way)
            for way, place in enumerate((below, above))
        ]

    def gcopies(part):
        return [
            (here.at[span], place.at[span], sends.at[part, way], gets.at[part, way], way)
            for here, places, sends, gets, span in (
                (code, (code_low, code_high), sp, rp, kinds(part)),
                (scale, (scale_low, scale_high), sq, rq, part),
            )
            for way, place in enumerate(places)
        ]

    def along_z(copies, act):
        for here, place, send, get, way in copies:
            copy = pltpu.make_async_remote_copy(
                src_ref=here, dst_ref=place, send_sem=send, recv_sem=get,
                device_id=(group, lower if way else upper), device_id_type=MESH,
            )
            there = has_lower if (act == "wait_recv") != (way == 1) else has_upper
            pl.when(there)(getattr(copy, act))

    def pack(chunk):
        for plane in range(parts[chunk].start, parts[chunk].start + parts[chunk].size):
            block = state_ref[plane - 1] if plane else coef_ref[...]
            send1[plane] = dot(chosen, block).astype(BF16)
        part = parts[chunk]
        recv1[part, xmine, :] = send1[part, xmine, :]

    def spread(chunk):
        send(chunk, send1, recv1, xmine, list(zip(xblocks, xdevices)), s1, r1)

    def turn(chunk):
        wait(chunk, recv1, xrows, r1)
        for plane in range(parts[chunk].start, parts[chunk].start + parts[chunk].size):
            send2[plane] = dot(swap, recv1[plane]).astype(BF16)
        send(chunk, send2, arrived, ymine, list(zip(yblocks, ydevices)), s2, r2)
        part = parts[chunk]
        arrived[part, ymine, :] = send2[part, ymine, :]

    def forward(chunk):
        wait(chunk, arrived, yrows, r2)
        along_z(zcopies(chunk), "start")

    def start(chunk):
        pack(chunk)
        spread(chunk)

    loads[1].wait()
    pack(0)
    pl.semaphore_wait(
        barrier, across + along - 2 + has_upper.astype(jnp.int32) + has_lower.astype(jnp.int32)
    )
    spread(0)
    loads[2].wait()
    start(1)

    for chunk in range(2, 1 + EARLY):
        start(chunk)
    turn(0)

    def prepare():
        loads[3].wait()
        loads[4].wait()
        for face in range(6):
            pick2[face] = jnp.where(lists_ref[face] == row, 1.0, 0.0).T.astype(BF16)

        @pl.when(jnp.logical_not(has_lower))
        def _():
            below[...] = jnp.zeros_like(below)
            scale_low[...] = jnp.zeros_like(scale_low)
            code_low[...] = jnp.zeros_like(code_low)

        @pl.when(jnp.logical_not(has_upper))
        def _():
            above[...] = jnp.zeros_like(above)
            scale_high[...] = jnp.zeros_like(scale_high)
            code_high[...] = jnp.zeros_like(code_high)

    def placing(field):
        lead = ones_where(iota((8, cells), 1) == 0)
        value = lax.dot_general(lead, field, (((1,), (1,)), ((), ())), preferred_element_type=F32)
        there = ones_where(value > 0.25)
        place = dot(there, earlier)[0:1].astype(jnp.int32)
        return ones_where((place == row) & (there[0:1] > 0))

    def first_near(plane):
        block = arrived[plane]
        field = dot(pick1[0], block)
        near = beside(field, [dot(pick1[face + 1], block) for face in range(4)])
        return field, near + (dot(pick1[5], below[plane]), dot(pick1[6], above[plane]))

    def setup():
        order = placing(arrived[0])
        pick1[0] = order
        for face in range(4):
            pick1[face + 1] = dot(pick2[face], order).astype(BF16)
        pick1[5] = dot(pick2[4], placing(below[0])).astype(BF16)
        pick1[6] = dot(pick2[5], placing(above[0])).astype(BF16)

        field, near = first_near(0)
        summed = None
        for face in range(6):
            part = 0.5 * (field + near[face])
            weight[face] = part
            summed = part if summed is None else summed + part
        total[...] = summed

    def relax(kind, rhs, near, faces):
        flow = None
        for face, value in zip(faces, near):
            part = weight[face] * value
            flow = part if flow is None else flow + part
        factor = lewis_ref[kind]
        share = 1.0 / (1.0 + factor * total[...])
        return rhs * share + (factor * share) * flow if rhs is not None else (factor * share) * flow

    def relax_first(chunk, kind):
        rhs, near = first_near(kind + 1)
        kept[kind] = rhs.astype(BF16)
        phi = relax(kind, rhs, near, range(6))
        out_ref[kind] = phi
        largest = jnp.maximum(jnp.max(jnp.abs(phi), axis=1, keepdims=True), 1e-30)
        unit = (largest * (1.01 / TOP)).astype(BF16).astype(F32)
        code[kind] = jnp.round(phi * (1.0 / unit)).astype(jnp.int32).astype(jnp.int16)
        across_lanes = dot(jnp.ones((16, slots), BF16), jnp.where(row == col, unit, 0.0).astype(BF16))
        scale[chunk, pl.ds(kind - kinds(chunk).start, 1), :] = across_lanes[:1]

    def sweep(chunk):
        along_z(zcopies(chunk), "wait_recv")
        if chunk == 0:
            setup()
        part = kinds(chunk)
        if part.size:
            pl.loop(part.start, part.start + part.size)(functools.partial(relax_first, chunk))
            along_z(gcopies(chunk), "start")

    for step in range(1, chunks + 1 + BEHIND):
        if step + EARLY < chunks:
            start(step + EARLY)
        if step < chunks:
            turn(step)
        if step <= chunks:
            forward(step - 1)
        if step == 1:
            prepare()
        if step > BEHIND:
            sweep(step - 1 - BEHIND)

    for chunk in range(chunks):
        wait(chunk, send1, xrows, s1)
        wait(chunk, send2, yrows, s2)
        along_z(zcopies(chunk), "wait_send")

    @pl.loop(0, species)
    def _(kind):
        phi = out_ref[kind]
        head, tail = split(phi)
        pair = jnp.concatenate([head, tail], axis=0)
        near = beside(
            phi, [dot(jnp.concatenate([pick2[face], pick2[face]], axis=1), pair) for face in range(4)]
        )
        out_ref[kind] = relax(kind, kept[kind].astype(F32), near, range(4))

    def last(chunk, kind):
        ends = ()
        for face, codes, scales in ((4, code_low, scale_low), (5, code_high, scale_high)):
            value = codes[kind].astype(jnp.int32).astype(F32)
            high = jnp.floor(value * (1.0 / 256.0) + 0.5)
            pair = jnp.concatenate([high.astype(BF16), (value - 256.0 * high).astype(BF16)], axis=0)
            hot = pick2[face].astype(F32) * scales[chunk, pl.ds(kind - kinds(chunk).start, 1), :]
            ends += (dot(jnp.concatenate([(256.0 * hot).astype(BF16), hot.astype(BF16)], axis=1), pair),)
        out_ref[kind] = out_ref[kind] + relax(kind, None, ends, (4, 5))

    busy = [chunk for chunk in range(chunks) if kinds(chunk).size]
    for chunk in busy:
        along_z(gcopies(chunk), "wait_recv")
        part = kinds(chunk)
        pl.loop(part.start, part.start + part.size)(functools.partial(last, chunk))
    for chunk in busy:
        along_z(gcopies(chunk), "wait_send")


def per_device(across, along, members, state, coef, new_group, face_lists, lewis):
    _, _, slots, species, cells = state.shape
    chunks = len(SIZES)
    whole = pl.BlockSpec(memory_space=pltpu.VMEM)
    far = pl.BlockSpec(memory_space=pltpu.HBM)
    dma = pltpu.SemaphoreType.DMA
    planes = (species + 1, slots, cells)
    out = pl.pallas_call(
        functools.partial(kernel, across, along, members, SIZES),
        out_shape=pltpu.VMEM((species, slots, cells), F32),
        in_specs=[far] * 5,
        out_specs=whole,
        scratch_shapes=[
            pltpu.VMEM((1, slots), jnp.int32),
            pltpu.VMEM((6, 1, slots), jnp.int32),
            pltpu.SMEM((species,), F32),
            pltpu.VMEM((slots, cells), BF16),
            pltpu.VMEM((species, slots, cells), BF16),
            pltpu.VMEM(planes, BF16),
            pltpu.VMEM(planes, BF16),
            pltpu.VMEM(planes, BF16),
            pltpu.VMEM(planes, BF16),
            pltpu.VMEM(planes, BF16),
            pltpu.VMEM(planes, BF16),
            pltpu.VMEM((species, slots, cells), BF16),
            pltpu.VMEM((6, slots, cells), F32),
            pltpu.VMEM((slots, cells), F32),
            pltpu.VMEM((7, slots, slots), BF16),
            pltpu.VMEM((6, slots, slots), BF16),
            pltpu.VMEM((species, slots, cells), jnp.int16),
            pltpu.VMEM((species, slots, cells), jnp.int16),
            pltpu.VMEM((species, slots, cells), jnp.int16),
            pltpu.VMEM((chunks, 8, slots), F32),
            pltpu.VMEM((chunks, 8, slots), F32),
            pltpu.VMEM((chunks, 8, slots), F32),
            dma((5,)),
            dma((chunks,)),
            dma((chunks,)),
            dma((chunks,)),
            dma((chunks,)),
            dma((chunks, 2)),
            dma((chunks, 2)),
            dma((chunks, 2)),
            dma((chunks, 2)),
            dma((chunks, 2)),
            dma((chunks, 2)),
        ],
        compiler_params=pltpu.CompilerParams(
            collective_id=0, has_side_effects=True, vmem_limit_bytes=60 * 2**20
        ),
        name="regrid_and_sweep",
    )(
        new_group[0],
        jnp.transpose(face_lists[0], (1, 0, 2)),
        lewis,
        coef[0, 0],
        jnp.transpose(state[0, 0], (1, 0, 2)),
    )
    return jnp.transpose(out, (1, 0, 2))[None, None]


def solution(mesh):
    groups, members = mesh.shape["group"], mesh.shape["member"]
    across = math.isqrt(groups)
    return jax.shard_map(
        functools.partial(per_device, across, groups // across, members),
        mesh=mesh,
        in_specs=(
            P("group", "member", None, None, None),
            P("group", "member", None, None),
            P("group", "member", None),
            P("group", "member", None, None),
            P(),
        ),
        out_specs=P("group", "member", None, None, None),
        check_vma=False,
    )
```
